32 devices in a mesh: sym: 4 (over y, core), rows: 8 (over z, x).
Axes of the slice: x: 2, y: 2, z: 4, core: 2. Of those that a mesh axis runs over, the one named last changes fastest.
Arguments:
- coeffs: bfloat16 [4096, 4096], P('rows', 'sym'), may hold values from -6 to 6
- beta_op: bfloat16 [4, 1024, 1024], P('sym'), may hold values from -0.1875 to 0.1875
- mix_op: bfloat16 [4, 4, 8, 128, 128], P('sym'), may hold values from -0.125 to 0.125
- pair_op: bfloat16 [8, 128, 128], replicated, may hold values from -0.1875 to 0.1875
- send_list: int32 [8, 8, 2], replicated, may hold values from -1 to 3, as said below
- mix_slot: int32 [32, 16], replicated, may hold values from 0 to 15, as said below
- mix_sign: int32 [32, 16], replicated, may hold values from 0 to 1
- mix_pair: int32 [32, 16], replicated, may hold values from 0 to 3
- aa_src: int32 [32, 8], replicated, may hold values from 0 to 31
- aa_sign: int32 [32, 8], replicated, may hold values from 0 to 1
- aa_pair: int32 [32, 8], replicated, may hold values from 0 to 7
Outputs:
- sigma: float32 [4096, 4096], P('rows', 'sym')
The draws below stay inside these ranges and needn't reach their ends.
Inputs may be any that keep to these rules, and one draw needn't show every extreme that they name: send_list[s, r, c] is the block, counted within device s's own 4 alpha blocks, that s sends to device r in slot c, or -1 for an empty slot; live slots of a pair come first and hold distinct blocks; every device sends at least one block to itself; in every draw some device receives 2 blocks from every device. mix_slot[P, l] = s * 2 + c names slot c of send_list[s, P // 4], always a live one; every live slot sent to a device is named by some entry of that device's destination blocks.
All inputs are finite; a program needn't handle non-finite values.
Results may differ from the reference program's by a relative error of at most 0.0075.
Values may be sent and summed in bfloat16 or wider, within the bound.
A program may use at most 128 MiB of HBM per device.

```python
import jax
import jax.numpy as jnp
from jax import lax

TILE = 128
BT = 8
ABLK = 4
CAP = 2
ENTRIES = 16
KA = 8
NPA = 8
RANKS = 8
SECTORS = 4
NBLK = 32
NA = 4096
BS = 1024
NB = 4096


def routing(key):
    base = jax.random.fold_in(key, 4021)
    key_list = jax.random.split(base, 6)
    full_dest = jax.random.randint(key_list[0], (), 0, RANKS)
    src_ids = jnp.arange(RANKS)[:, None]
    dst_ids = jnp.arange(RANKS)[None, :]
    counts = jax.random.randint(key_list[1], (RANKS, RANKS), 0, CAP + 1)
    counts = jnp.where(dst_ids == full_dest, CAP, counts)
    counts = jnp.where(src_ids == dst_ids, jnp.maximum(counts, 1), counts)
    scores = jax.random.randint(key_list[2], (RANKS, RANKS, ABLK), 0, 1 << 20) * ABLK + jnp.arange(ABLK)
    block_order = jnp.argsort(scores, axis=-1, stable=True)[:, :, :CAP]
    slot_ids = jnp.arange(CAP)
    live_slot = slot_ids[None, None, :] < counts[:, :, None]
    sends = jnp.where(live_slot, block_order, -1).astype(jnp.int32)
    slot_total = RANKS * CAP
    live_dest = jnp.transpose(live_slot, (1, 0, 2)).reshape(RANKS, slot_total)
    jitter = jax.random.randint(key_list[3], (RANKS, slot_total), 0, 1 << 20) * slot_total + jnp.arange(slot_total)
    ranked = jnp.argsort(jnp.where(live_dest, -jitter - 1, jitter), axis=-1, stable=True)
    live_count = jnp.sum(live_dest.astype(jnp.int32), axis=-1)
    entry_total = ABLK * ENTRIES
    entry_ids = jnp.arange(entry_total)[None, :]
    picked = jax.random.randint(key_list[4], (RANKS, entry_total), 0, 1 << 20) % live_count[:, None]
    positions = jnp.where(entry_ids < live_count[:, None], entry_ids, picked)
    chosen = jnp.take_along_axis(ranked, positions, axis=1)
    shuffle = jnp.argsort(jax.random.randint(key_list[5], (RANKS, entry_total), 0, 1 << 20) * entry_total + entry_ids, axis=-1, stable=True)
    chosen = jnp.take_along_axis(chosen, shuffle, axis=1)
    return (sends, chosen.reshape(RANKS * ABLK, ENTRIES).astype(jnp.int32))


def draw_send_list(key, part):
    return routing(key)[0]


def draw_mix_slot(key, part):
    return routing(key)[1]


def place_ends(result, stream_key, low, high):
    index_at = [jax.random.randint(jax.random.fold_in(stream_key, axis), (), 0, length) for axis, length in enumerate(result.shape)]
    longest = result.shape.index(max(result.shape))
    neighbour = index_at[:longest] + [(index_at[longest] + 1) % result.shape[longest]] + index_at[longest + 1:]
    return result.at[tuple(index_at)].set(low).at[tuple(neighbour)].set(high)


def level_of(stream_key, extent, shards, low, top_value):
    def one(dim, parts):
        steps = jax.random.uniform(jax.random.fold_in(jax.random.fold_in(stream_key, 6), dim), (parts,), jnp.float32, low / len(shards), top_value / len(shards))
        return jnp.repeat(jnp.exp(steps), extent[dim] // parts).reshape((-1,) + (1,) * (len(extent) - dim - 1))

    gain = one(*shards[0])
    for cut in shards[1:]:
        gain = gain * one(*cut)
    return gain


def scatter_about(own_key, shape, deviation, most, cuts=(), kind=jnp.bfloat16):
    level = level_of(own_key, shape, cuts, -0.22, 0.18) if cuts else 1.0
    values = jax.random.normal(own_key, shape, jnp.float32) * deviation * level
    return jnp.minimum(jnp.maximum(values, -most), most).astype(kind)


def setup_inputs(seed: int = 0) -> dict:
    seeds = jax.random.split(jax.random.key(seed), 12)
    coeffs = scatter_about(seeds[0], (NA, NB), 1.0, 6.0, ((0, 8), (1, 4)))
    beta_op = scatter_about(seeds[1], (SECTORS, BS, BS), BS ** -0.5, 0.1875, ((0, 4),))
    mix_op = scatter_about(seeds[2], (SECTORS, SECTORS, BT, TILE, TILE), (TILE * ENTRIES) ** -0.5, 0.125, ((0, 4),))
    pair_op = scatter_about(seeds[3], (NPA, TILE, TILE), (TILE * KA) ** -0.5, 0.1875)
    send_list = draw_send_list(jax.random.fold_in(seeds[11], 71), 0)
    mix_slot = draw_mix_slot(jax.random.fold_in(seeds[11], 71), 0)
    mix_sign = place_ends(jax.random.randint(seeds[6], (NBLK, ENTRIES), 0, 2), jax.random.fold_in(seeds[6], 1), 0, 1).astype(jnp.int32)
    mix_pair = place_ends(jax.random.randint(seeds[7], (NBLK, ENTRIES), 0, SECTORS), jax.random.fold_in(seeds[7], 1), 0, SECTORS - 1).astype(jnp.int32)
    aa_src = place_ends(jax.random.randint(seeds[8], (NBLK, KA), 0, NBLK), jax.random.fold_in(seeds[8], 1), 0, NBLK - 1).astype(jnp.int32)
    aa_sign = place_ends(jax.random.randint(seeds[9], (NBLK, KA), 0, 2), jax.random.fold_in(seeds[9], 1), 0, 1).astype(jnp.int32)
    aa_pair = place_ends(jax.random.randint(seeds[10], (NBLK, KA), 0, NPA), jax.random.fold_in(seeds[10], 1), 0, NPA - 1).astype(jnp.int32)
    return {"coeffs": coeffs, "beta_op": beta_op, "mix_op": mix_op, "pair_op": pair_op, "send_list": send_list, "mix_slot": mix_slot, "mix_sign": mix_sign, "mix_pair": mix_pair, "aa_src": aa_src, "aa_sign": aa_sign, "aa_pair": aa_pair}


def reround(values):
    narrow = lax.optimization_barrier(values.astype(jnp.bfloat16))
    return narrow.astype(jnp.float32)


def reference(coeffs, beta_op, mix_op, pair_op, send_list, mix_slot, mix_sign, mix_pair, aa_src, aa_sign, aa_pair):
    blocks = coeffs.reshape(NBLK, TILE, NB)
    pieces = []
    for sector in range(SECTORS):
        pieces.append(jnp.dot(coeffs[:, sector * BS:(sector + 1) * BS], beta_op[sector], preferred_element_type=jnp.float32))
    beta_part = jnp.concatenate(pieces, axis=1)

    slot_src = (mix_slot // CAP).astype(jnp.int32)
    slot_pos = (mix_slot % CAP).astype(jnp.int32)
    dest_rank = (jnp.arange(NBLK, dtype=jnp.int32) // ABLK)[:, None]
    source = slot_src * ABLK + send_list[slot_src, dest_rank, slot_pos]
    mixed_sign = (1 - 2 * mix_sign).astype(jnp.float32)
    pair_ids = jnp.arange(SECTORS, dtype=jnp.int32)
    flipped = jnp.bitwise_xor(pair_ids[:, None], pair_ids[None, :])
    chosen_ops = mix_op[flipped, pair_ids[None, :]].astype(jnp.float32)

    def mixed_block(inputs):
        src_row, sign_row, pair_row = inputs
        picked = blocks[src_row].astype(jnp.float32)
        weights = sign_row[None, :] * (pair_row[None, :] == pair_ids[:, None]).astype(jnp.float32)
        combo = reround(jnp.einsum('gl,lin->gin', weights, picked))
        combo = combo.reshape(SECTORS, TILE, SECTORS, BT, TILE)
        selected = combo[pair_ids[None, :], :, flipped]
        terms = reround(jnp.einsum('dgitk,dgtkj->dgitj', selected, chosen_ops))
        summed = jnp.sum(terms, axis=1)
        return jnp.transpose(summed, (1, 0, 2, 3)).reshape(TILE, NB)

    mixed_part = lax.map(mixed_block, (source, mixed_sign, mix_pair)).reshape(NA, NB)

    alpha_sign = (1 - 2 * aa_sign).astype(jnp.float32)
    operator_ids = jnp.arange(NPA, dtype=jnp.int32)
    pair_float = pair_op.astype(jnp.float32)

    def alpha_block(inputs):
        src_row, sign_row, pair_row = inputs
        picked = blocks[src_row].astype(jnp.float32)
        weights = sign_row[None, :] * (pair_row[None, :] == operator_ids[:, None]).astype(jnp.float32)
        combo = reround(jnp.einsum('gk,kin->gin', weights, picked))
        return jnp.einsum('gij,gjn->in', pair_float, combo)

    alpha_part = lax.map(alpha_block, (aa_src, alpha_sign, aa_pair)).reshape(NA, NB)
    return beta_part + alpha_part + mixed_part
```

```python
import functools

import jax
import jax.numpy as jnp
from jax import lax
from jax.experimental import pallas as pl
from jax.experimental.pallas import tpu as pltpu
from jax.sharding import PartitionSpec as P

TILE = 128
BT = 8
CAP = 2
NPA = 8
CHUNK = 32
MESH = pl.DeviceIdType.MESH


def spread(
    coeffs,
    beta_op,
    mix_op,
    pair_op,
    send_list,
    mix_slot,
    mix_sign,
    mix_pair,
    aa_src,
    aa_sign,
    aa_pair,
):
    rows_here, beta_here = coeffs.shape
    ablk = rows_here // TILE
    sectors = lax.axis_size("sym")
    rank_count = lax.axis_size("rows")
    sector = lax.axis_index("sym")
    my_rank = lax.axis_index("rows")
    block_count = aa_src.shape[0]
    total_rows = block_count * TILE
    col_width = beta_here // rank_count
    local_term = jnp.dot(coeffs, beta_op[0], preferred_element_type=jnp.float32)
    flipped = coeffs.T
    columns = lax.all_to_all(flipped, "rows", split_axis=0, concat_axis=1, tiled=True)
    col_blocks = columns.reshape(col_width, block_count, TILE)
    picked = jnp.take(col_blocks, aa_src, axis=1)
    operator_ids = jnp.arange(NPA, dtype=jnp.int32)
    aa_weight = (
        (1 - 2 * aa_sign)[:, :, None]
        * (aa_pair[:, :, None] == operator_ids[None, None, :]).astype(jnp.int32)
    ).astype(jnp.bfloat16)
    combined = jnp.einsum(
        "cpki,pkg->cpgi", picked, aa_weight, preferred_element_type=jnp.float32
    ).astype(jnp.bfloat16)
    alpha_part = jnp.einsum(
        "cpgj,gij->cpi", combined, pair_op, preferred_element_type=jnp.float32
    ).reshape(col_width, total_rows)
    returned = lax.all_to_all(
        alpha_part.astype(jnp.bfloat16), "rows", split_axis=1, concat_axis=0, tiled=True
    ).astype(alpha_part.dtype)
    dest_ids = jnp.arange(sectors, dtype=jnp.int32)
    pair_of = jnp.bitwise_xor(sector, dest_ids)
    operators = jnp.take(mix_op[0], pair_of, axis=0)
    sign_all = (1 - 2 * mix_sign).astype(jnp.float32)
    my_sends = lax.dynamic_index_in_dim(send_list, my_rank, 0, keepdims=False)
    blocks = coeffs.reshape(ablk, TILE, beta_here)
    taken = jnp.take(blocks, jnp.maximum(my_sends, 0), axis=0)
    outgoing = jnp.where((my_sends >= 0)[:, :, None, None], taken, jnp.zeros_like(taken))
    arrived = lax.all_to_all(outgoing, "rows", split_axis=0, concat_axis=0, tiled=True)
    slot_total = rank_count * CAP
    arrived = arrived.reshape(slot_total, TILE * beta_here)
    my_slots = lax.dynamic_slice_in_dim(mix_slot, my_rank * ablk, ablk, 0)
    my_signs = lax.dynamic_slice_in_dim(sign_all, my_rank * ablk, ablk, 0)
    my_pairs = lax.dynamic_slice_in_dim(mix_pair, my_rank * ablk, ablk, 0)
    weight = my_signs[None, :, :] * (my_pairs[None, :, :] == pair_of[:, None, None]).astype(
        jnp.float32
    )
    onehot = (
        my_slots[:, :, None] == jnp.arange(slot_total, dtype=jnp.int32)[None, None, :]
    ).astype(jnp.float32)
    mixing = (
        jnp.einsum("dpl,pls->dps", weight, onehot)
        .astype(jnp.bfloat16)
        .reshape(sectors * ablk, slot_total)
    )
    inputs = jnp.dot(mixing, arrived, preferred_element_type=jnp.float32).astype(jnp.bfloat16)
    inputs = inputs.reshape(sectors, rows_here, BT, TILE)
    products = jnp.einsum(
        "drtk,dtkj->drtj", inputs, operators, preferred_element_type=jnp.float32
    )
    mixed = lax.psum_scatter(
        products.reshape(sectors * rows_here, beta_here).astype(jnp.bfloat16),
        "sym",
        scatter_dimension=0,
        tiled=True,
    ).astype(jnp.float32)
    return local_term + returned.T + mixed


def kernel(
    ranks,
    coeffs,
    beta_op,
    mix_op,
    pair_op,
    mix_src,
    mix_weight,
    aa_src,
    aa_op,
    out,
    cols,
    mine,
    beta,
    pairs,
    mops,
    combo,
    base,
    across,
    core_out,
    core_in,
    y_out,
    y_in,
    back_out,
    back_in,
    local_sem,
    go_send,
    go_recv,
    core_send,
    core_recv,
    y_send,
    y_recv,
    back_send,
    back_recv,
):
    ablk, _, beta_here = coeffs.shape
    entries = mix_src.shape[1]
    ka = aa_src.shape[1]
    npa = pair_op.shape[0]
    me = lax.axis_index("rows")
    sym = lax.axis_index("sym")
    core_mate = sym + 1 - 2 * lax.rem(sym, 2)
    y_mate = lax.rem(sym + 2, 4)

    def block_cols(r):
        return pl.ds(pl.multiple_of(r * TILE, TILE), TILE)

    def blocks_of(r):
        return pl.ds(r * ablk, ablk)

    load_mine = pltpu.make_async_copy(coeffs, mine, local_sem.at[0])
    load_beta = pltpu.make_async_copy(beta_op.at[0], beta, local_sem.at[1])
    load_mops = pltpu.make_async_copy(mix_op.at[0, :, me], mops, local_sem.at[2])
    load_own = pltpu.make_async_copy(
        coeffs.at[:, :, block_cols(me)], cols.at[blocks_of(me)], local_sem.at[3]
    )
    load_mine.start()
    load_beta.start()
    load_mops.start()
    load_own.start()

    barrier = pltpu.get_barrier_semaphore()
    for i in range(1, ranks):
        pl.semaphore_signal(
            barrier, inc=1, device_id={"rows": lax.rem(me + i, ranks)}, device_id_type=MESH
        )
    pl.semaphore_signal(barrier, inc=1, device_id={"sym": core_mate}, device_id_type=MESH)
    pl.semaphore_signal(barrier, inc=1, device_id={"sym": y_mate}, device_id_type=MESH)
    pl.semaphore_wait(barrier, ranks + 1)

    def go(i):
        r = lax.rem(me + 1 + i, ranks)
        return pltpu.make_async_remote_copy(
            src_ref=coeffs.at[:, :, block_cols(r)],
            dst_ref=cols.at[blocks_of(me)],
            send_sem=go_send.at[i],
            recv_sem=go_recv.at[i],
            device_id={"rows": r},
            device_id_type=MESH,
        )

    def go_in(i):
        r = lax.rem(me + 2 * ranks - 1 - i, ranks)
        return pltpu.make_async_remote_copy(
            src_ref=coeffs.at[:, :, block_cols(r)],
            dst_ref=cols.at[blocks_of(r)],
            send_sem=go_send.at[i],
            recv_sem=go_recv.at[i],
            device_id={"rows": r},
            device_id_type=MESH,
        )

    for i in range(ranks - 1):
        go(i).start()

    for k in range(npa):
        pairs[k] = pair_op[k]
        pairs[npa + k] = -pair_op[k]

    load_mine.wait()
    load_beta.wait()
    width = 2 * TILE

    @pl.loop(0, beta_here // width)
    def _(n):
        at = pl.ds(pl.multiple_of(n * width, width), width)

        for m in range(ablk):
            out[m, :, at] = jnp.dot(
                mine[m], beta[:, at], preferred_element_type=jnp.float32
            )

    load_mops.wait()
    load_own.wait()
    for i in range(ranks - 1):
        go_in(i).wait_recv()
    for i in range(ranks - 1):
        go(i).wait_send()

    def core_copy(i):
        return pltpu.make_async_remote_copy(
            src_ref=core_out.at[i],
            dst_ref=core_in.at[i],
            send_sem=core_send.at[i],
            recv_sem=core_recv.at[i],
            device_id={"sym": core_mate},
            device_id_type=MESH,
        )

    def y_copy(i):
        return pltpu.make_async_remote_copy(
            src_ref=y_out.at[i],
            dst_ref=y_in.at[i],
            send_sem=y_send.at[i],
            recv_sem=y_recv.at[i],
            device_id={"sym": y_mate},
            device_id_type=MESH,
        )

    def back_copy(i):
        return pltpu.make_async_remote_copy(
            src_ref=back_out.at[i],
            dst_ref=back_in.at[i],
            send_sem=back_send.at[i],
            recv_sem=back_recv.at[i],
            device_id={"rows": lax.rem(me + 1 + i, ranks)},
            device_id_type=MESH,
        )

    def compute(i):
        r = lax.rem(me + 1 + i, ranks)

        def one(b, carry):
            p = r * ablk + b
            alpha = jnp.dot(
                jnp.concatenate([pairs[aa_op[p, k]] for k in range(ka)], axis=1),
                jnp.concatenate([cols[aa_src[p, k]] for k in range(ka)], axis=0),
                preferred_element_type=jnp.float32,
            )
            sources = [mix_src[p, l] for l in range(entries)]
            for c in range(TILE // CHUNK):
                total = [jnp.zeros((CHUNK, TILE), jnp.float32) for _ in range(4)]
                for l in range(entries):
                    x = cols[sources[l], c * CHUNK : (c + 1) * CHUNK, :].astype(jnp.float32)
                    for g in range(4):
                        total[g] = total[g] + mix_weight[p, g * entries + l] * x
                for g in range(4):
                    combo[g, c * CHUNK : (c + 1) * CHUNK, :] = total[g].astype(jnp.bfloat16)
            term = [
                jnp.dot(combo[g], mops[g], preferred_element_type=jnp.float32).astype(
                    jnp.bfloat16
                )
                for g in range(4)
            ]
            base[i, b] = alpha + term[0].astype(jnp.float32)
            across[i, b] = term[2]
            core_out[i, 0, b] = term[1]
            core_out[i, 1, b] = term[3]
            return carry

        lax.fori_loop(0, ablk, one, 0)

    def step(i, carry):
        @pl.when(i < ranks)
        def _():
            compute(i)
            core_copy(i).start()

        @pl.when((i >= 1) & (i < ranks + 1))
        def _():
            j = i - 1
            core_copy(j).wait_recv()
            y_out[j] = (
                across[j].astype(jnp.float32) + core_in[j, 1].astype(jnp.float32)
            ).astype(jnp.bfloat16)
            y_copy(j).start()

        @pl.when(i >= 2)
        def _():
            j = i - 2
            y_copy(j).wait_recv()
            back_out[j] = (
                base[j] + core_in[j, 0].astype(jnp.float32) + y_in[j].astype(jnp.float32)
            ).astype(jnp.bfloat16)

            @pl.when(j < ranks - 1)
            def _():
                back_copy(j).start()

        return carry

    lax.fori_loop(0, ranks + 2, step, 0)

    at = block_cols(me)
    out[:, :, at] = out[:, :, at] + back_out[ranks - 1].astype(jnp.float32)

    def finish(i, carry):
        back_copy(i).wait_recv()
        here = block_cols(lax.rem(me + 2 * ranks - 1 - i, ranks))
        out[:, :, here] = out[:, :, here] + back_in[i].astype(jnp.float32)
        return carry

    lax.fori_loop(0, ranks - 1, finish, 0)

    def drain(i, carry):
        core_copy(i).wait_send()
        y_copy(i).wait_send()

        @pl.when(i < ranks - 1)
        def _():
            back_copy(i).wait_send()

        return carry

    lax.fori_loop(0, ranks, drain, 0)


def plan(ablk, send_list, mix_slot, mix_sign, mix_pair, aa_sign, aa_pair, sectors, npa):
    ranks, _, cap = send_list.shape
    slots = jnp.arange(ranks * cap, dtype=jnp.int32)
    table = jnp.transpose(send_list, (1, 0, 2)).reshape(ranks, ranks * cap)
    table = table + (slots // cap * ablk)[None, :]
    table = jnp.repeat(table, ablk, axis=0)
    hit = mix_slot[:, :, None] == slots[None, None, :]
    mix_src = jnp.sum(jnp.where(hit, table[:, None, :], 0), axis=2)
    which = jnp.arange(sectors, dtype=jnp.int32)[None, :, None]
    sign = (1 - 2 * mix_sign)[:, None, :]
    weight = jnp.where(mix_pair[:, None, :] == which, sign, 0).astype(jnp.float32)
    return mix_src, weight.reshape(mix_slot.shape[0], -1), aa_sign * npa + aa_pair


def fused(
    ranks,
    coeffs,
    beta_op,
    mix_op,
    pair_op,
    send_list,
    mix_slot,
    mix_sign,
    mix_pair,
    aa_src,
    aa_sign,
    aa_pair,
):
    rows_here, beta_here = coeffs.shape
    ablk = rows_here // TILE
    bf16, f32 = jnp.bfloat16, jnp.float32
    sectors = mix_op.shape[1]
    npa = pair_op.shape[0]
    mix_src, mix_weight, aa_op = plan(
        ablk, send_list, mix_slot, mix_sign, mix_pair, aa_sign, aa_pair, sectors, npa
    )
    piece = (ranks, ablk, TILE, TILE)
    vmem, smem, anywhere = pltpu.VMEM, pltpu.SMEM, pl.ANY
    dma = pltpu.SemaphoreType.DMA
    result = pl.pallas_call(
        functools.partial(kernel, ranks),
        out_shape=jax.ShapeDtypeStruct((ablk, TILE, beta_here), f32),
        in_specs=[pl.BlockSpec(memory_space=anywhere)] * 3
        + [pl.BlockSpec(memory_space=vmem)]
        + [pl.BlockSpec(memory_space=smem)] * 4,
        out_specs=pl.BlockSpec(memory_space=vmem),
        scratch_shapes=[
            vmem((ranks * ablk, TILE, TILE), bf16),
            vmem((ablk, TILE, beta_here), bf16),
            vmem((beta_here, beta_here), bf16),
            vmem((2 * npa, TILE, TILE), bf16),
            vmem((sectors, TILE, TILE), bf16),
            vmem((sectors, TILE, TILE), bf16),
            vmem(piece, f32),
            vmem(piece, bf16),
            vmem((ranks, 2, ablk, TILE, TILE), bf16),
            vmem((ranks, 2, ablk, TILE, TILE), bf16),
            vmem(piece, bf16),
            vmem(piece, bf16),
            vmem(piece, bf16),
            vmem(piece, bf16),
            dma((4,)),
        ]
        + [dma((ranks,))] * 8,
        compiler_params=pltpu.CompilerParams(
            collective_id=0, has_side_effects=True, vmem_limit_bytes=56 * 1024 * 1024
        ),
        cost_estimate=pl.CostEstimate(
            flops=6 * rows_here * beta_here * beta_here,
            bytes_accessed=12 * rows_here * beta_here,
            transcendentals=0,
        ),
    )(
        coeffs.reshape(ablk, TILE, beta_here),
        beta_op,
        mix_op,
        pair_op,
        mix_src,
        mix_weight,
        aa_src,
        aa_op,
    )
    return result.reshape(rows_here, beta_here)


def solution(mesh):
    ranks, sectors = mesh.shape["rows"], mesh.shape["sym"]

    def per_device(coeffs, *rest):
        whole_blocks = coeffs.shape[1] == ranks * TILE
        if sectors == 4 and whole_blocks:
            return fused(ranks, coeffs, *rest)
        return spread(coeffs, *rest)

    in_specs = (
        P("rows", "sym"),
        P("sym", None, None),
        P("sym", None, None, None, None),
    ) + (P(),) * 8
    return jax.shard_map(
        per_device, mesh=mesh, in_specs=in_specs, out_specs=P("rows", "sym"), check_vma=False
    )
```

```python
import functools

import jax
import jax.numpy as jnp
from jax import lax
from jax.experimental import pallas as pl
from jax.experimental.pallas import tpu as pltpu
from jax.sharding import PartitionSpec as P

TILE = 128
BT = 8
CAP = 2
NPA = 8
CHUNK = 32
MESH = pl.DeviceIdType.MESH


def spread(
    coeffs,
    beta_op,
    mix_op,
    pair_op,
    send_list,
    mix_slot,
    mix_sign,
    mix_pair,
    aa_src,
    aa_sign,
    aa_pair,
):
    rows_here, beta_here = coeffs.shape
    ablk = rows_here // TILE
    sectors = lax.axis_size("sym")
    rank_count = lax.axis_size("rows")
    sector = lax.axis_index("sym")
    my_rank = lax.axis_index("rows")
    block_count = aa_src.shape[0]
    total_rows = block_count * TILE
    col_width = beta_here // rank_count
    local_term = jnp.dot(coeffs, beta_op[0], preferred_element_type=jnp.float32)
    flipped = coeffs.T
    columns = lax.all_to_all(flipped, "rows", split_axis=0, concat_axis=1, tiled=True)
    col_blocks = columns.reshape(col_width, block_count, TILE)
    picked = jnp.take(col_blocks, aa_src, axis=1)
    operator_ids = jnp.arange(NPA, dtype=jnp.int32)
    aa_weight = (
        (1 - 2 * aa_sign)[:, :, None]
        * (aa_pair[:, :, None] == operator_ids[None, None, :]).astype(jnp.int32)
    ).astype(jnp.bfloat16)
    combined = jnp.einsum(
        "cpki,pkg->cpgi", picked, aa_weight, preferred_element_type=jnp.float32
    ).astype(jnp.bfloat16)
    alpha_part = jnp.einsum(
        "cpgj,gij->cpi", combined, pair_op, preferred_element_type=jnp.float32
    ).reshape(col_width, total_rows)
    returned = lax.all_to_all(
        alpha_part.astype(jnp.bfloat16), "rows", split_axis=1, concat_axis=0, tiled=True
    ).astype(alpha_part.dtype)
    dest_ids = jnp.arange(sectors, dtype=jnp.int32)
    pair_of = jnp.bitwise_xor(sector, dest_ids)
    operators = jnp.take(mix_op[0], pair_of, axis=0)
    sign_all = (1 - 2 * mix_sign).astype(jnp.float32)
    my_sends = lax.dynamic_index_in_dim(send_list, my_rank, 0, keepdims=False)
    blocks = coeffs.reshape(ablk, TILE, beta_here)
    taken = jnp.take(blocks, jnp.maximum(my_sends, 0), axis=0)
    outgoing = jnp.where((my_sends >= 0)[:, :, None, None], taken, jnp.zeros_like(taken))
    arrived = lax.all_to_all(outgoing, "rows", split_axis=0, concat_axis=0, tiled=True)
    slot_total = rank_count * CAP
    arrived = arrived.reshape(slot_total, TILE * beta_here)
    my_slots = lax.dynamic_slice_in_dim(mix_slot, my_rank * ablk, ablk, 0)
    my_signs = lax.dynamic_slice_in_dim(sign_all, my_rank * ablk, ablk, 0)
    my_pairs = lax.dynamic_slice_in_dim(mix_pair, my_rank * ablk, ablk, 0)
    weight = my_signs[None, :, :] * (my_pairs[None, :, :] == pair_of[:, None, None]).astype(
        jnp.float32
    )
    onehot = (
        my_slots[:, :, None] == jnp.arange(slot_total, dtype=jnp.int32)[None, None, :]
    ).astype(jnp.float32)
    mixing = (
        jnp.einsum("dpl,pls->dps", weight, onehot)
        .astype(jnp.bfloat16)
        .reshape(sectors * ablk, slot_total)
    )
    inputs = jnp.dot(mixing, arrived, preferred_element_type=jnp.float32).astype(jnp.bfloat16)
    inputs = inputs.reshape(sectors, rows_here, BT, TILE)
    products = jnp.einsum(
        "drtk,dtkj->drtj", inputs, operators, preferred_element_type=jnp.float32
    )
    mixed = lax.psum_scatter(
        products.reshape(sectors * rows_here, beta_here).astype(jnp.bfloat16),
        "sym",
        scatter_dimension=0,
        tiled=True,
    ).astype(jnp.float32)
    return local_term + returned.T + mixed


def kernel(
    ranks,
    coeffs,
    beta_op,
    mix_op,
    pair_op,
    send_list,
    mix_slot,
    mix_sign,
    mix_pair,
    aa_src,
    aa_sign,
    aa_pair,
    out,
    cols,
    mine,
    beta,
    mops,
    alphas,
    mixes,
    base,
    across,
    core_out,
    core_in,
    y_out,
    y_in,
    back_out,
    back_in,
    local_sem,
    go_send,
    go_recv,
    core_send,
    core_recv,
    y_send,
    y_recv,
    back_send,
    back_recv,
):
    ablk, _, beta_here = coeffs.shape
    entries = mix_slot.shape[0]
    ka = aa_src.shape[0]
    npa = pair_op.shape[0]
    sectors = mops.shape[0]
    me = lax.axis_index("rows")
    sym = lax.axis_index("sym")
    core_mate = sym + 1 - 2 * lax.rem(sym, 2)
    y_mate = lax.rem(sym + 2, 4)

    def block_cols(r):
        return pl.ds(pl.multiple_of(r * TILE, TILE), TILE)

    def blocks_of(r):
        return pl.ds(r * ablk, ablk)

    load_mine = pltpu.make_async_copy(coeffs, mine, local_sem.at[0])
    load_beta = pltpu.make_async_copy(beta_op.at[0], beta, local_sem.at[1])
    load_mops = pltpu.make_async_copy(mix_op.at[0, :, me], mops, local_sem.at[2])
    load_own = pltpu.make_async_copy(
        coeffs.at[:, :, block_cols(me)], cols.at[blocks_of(me)], local_sem.at[3]
    )
    load_mine.start()
    load_beta.start()
    load_mops.start()
    load_own.start()

    barrier = pltpu.get_barrier_semaphore()
    for i in range(1, ranks):
        pl.semaphore_signal(
            barrier, inc=1, device_id={"rows": lax.rem(me + i, ranks)}, device_id_type=MESH
        )
    pl.semaphore_signal(barrier, inc=1, device_id={"sym": core_mate}, device_id_type=MESH)
    pl.semaphore_signal(barrier, inc=1, device_id={"sym": y_mate}, device_id_type=MESH)
    pl.semaphore_wait(barrier, ranks + 1)

    def go(i):
        r = lax.rem(me + 1 + i, ranks)
        return pltpu.make_async_remote_copy(
            src_ref=coeffs.at[:, :, block_cols(r)],
            dst_ref=cols.at[blocks_of(me)],
            send_sem=go_send.at[i],
            recv_sem=go_recv.at[i],
            device_id={"rows": r},
            device_id_type=MESH,
        )

    def go_in(i):
        r = lax.rem(me + 2 * ranks - 1 - i, ranks)
        return pltpu.make_async_remote_copy(
            src_ref=coeffs.at[:, :, block_cols(r)],
            dst_ref=cols.at[blocks_of(r)],
            send_sem=go_send.at[i],
            recv_sem=go_recv.at[i],
            device_id={"rows": r},
            device_id_type=MESH,
        )

    for i in range(ranks - 1):
        go(i).start()

    load_mine.wait()
    load_beta.wait()
    width = 2 * TILE

    @pl.loop(0, beta_here // width)
    def _(n):
        at = pl.ds(pl.multiple_of(n * width, width), width)

        for m in range(ablk):
            out[m, :, at] = jnp.dot(
                mine[m], beta[:, at], preferred_element_type=jnp.float32
            )

    load_mops.wait()

    def products(r):
        stacked = pair_op[...].reshape(npa * TILE, TILE)

        def one(b, carry):
            block = r * ablk + b
            x = cols[block]
            alphas[block] = jnp.dot(
                stacked, x, preferred_element_type=jnp.float32
            ).reshape(npa, TILE, TILE)
            for g in range(sectors):
                mixes[block, g] = jnp.dot(x, mops[g], preferred_element_type=jnp.float32)
            return carry

        lax.fori_loop(0, ablk, one, 0)

    load_own.wait()
    products(me)

    def arrive(i, carry):
        go_in(i).wait_recv()
        products(lax.rem(me + 2 * ranks - 1 - i, ranks))
        return carry

    lax.fori_loop(0, ranks - 1, arrive, 0)
    for i in range(ranks - 1):
        go(i).wait_send()

    def core_copy(i):
        return pltpu.make_async_remote_copy(
            src_ref=core_out.at[i],
            dst_ref=core_in.at[i],
            send_sem=core_send.at[i],
            recv_sem=core_recv.at[i],
            device_id={"sym": core_mate},
            device_id_type=MESH,
        )

    def y_copy(i):
        return pltpu.make_async_remote_copy(
            src_ref=y_out.at[i],
            dst_ref=y_in.at[i],
            send_sem=y_send.at[i],
            recv_sem=y_recv.at[i],
            device_id={"sym": y_mate},
            device_id_type=MESH,
        )

    def back_copy(i):
        return pltpu.make_async_remote_copy(
            src_ref=back_out.at[i],
            dst_ref=back_in.at[i],
            send_sem=back_send.at[i],
            recv_sem=back_recv.at[i],
            device_id={"rows": lax.rem(me + 1 + i, ranks)},
            device_id_type=MESH,
        )

    def compute(i):
        r = lax.rem(me + 1 + i, ranks)

        def one(b, carry):
            p = r * ablk + b
            picks, signs = [], []
            for k in range(ka):
                picks.append((aa_src[k, p], aa_pair[k, p]))
                signs.append((1 - 2 * aa_sign[k, p]).astype(jnp.float32))
            finds, weights = [], []
            for l in range(entries):
                slot = mix_slot[l, p]
                s = lax.div(slot, CAP)
                pair = mix_pair[l, p]
                sign = (1 - 2 * mix_sign[l, p]).astype(jnp.float32)
                finds.append((s * ablk + send_list[s, slot - s * CAP, r], pair))
                weights.append([jnp.where(pair == g, sign, 0.0) for g in range(sectors)])
            for c in range(TILE // CHUNK):
                at = slice(c * CHUNK, (c + 1) * CHUNK)
                total = [jnp.zeros((CHUNK, TILE), jnp.float32) for _ in range(sectors)]
                for l in range(entries):
                    x = mixes[finds[l][0], finds[l][1], at, :]
                    for g in range(sectors):
                        total[g] = total[g] + weights[l][g] * x
                term = [t.astype(jnp.bfloat16) for t in total]
                across[i, b, at, :] = term[2]
                core_out[i, 0, b, at, :] = term[1]
                core_out[i, 1, b, at, :] = term[3]
                alpha = term[0].astype(jnp.float32)
                for k in range(ka):
                    alpha = alpha + signs[k] * alphas[picks[k][0], picks[k][1], at, :]
                base[i, b, at, :] = alpha
            return carry

        lax.fori_loop(0, ablk, one, 0)

    def step(i, carry):
        @pl.when(i < ranks)
        def _():
            compute(i)
            core_copy(i).start()

        @pl.when((i >= 1) & (i < ranks + 1))
        def _():
            j = i - 1
            core_copy(j).wait_recv()
            y_out[j] = (
                across[j].astype(jnp.float32) + core_in[j, 1].astype(jnp.float32)
            ).astype(jnp.bfloat16)
            y_copy(j).start()

        @pl.when(i >= 2)
        def _():
            j = i - 2
            y_copy(j).wait_recv()
            back_out[j] = (
                base[j] + core_in[j, 0].astype(jnp.float32) + y_in[j].astype(jnp.float32)
            ).astype(jnp.bfloat16)

            @pl.when(j < ranks - 1)
            def _():
                back_copy(j).start()

        return carry

    lax.fori_loop(0, ranks + 2, step, 0)

    at = block_cols(me)
    out[:, :, at] = out[:, :, at] + back_out[ranks - 1].astype(jnp.float32)

    def finish(i, carry):
        back_copy(i).wait_recv()
        here = block_cols(lax.rem(me + 2 * ranks - 1 - i, ranks))
        out[:, :, here] = out[:, :, here] + back_in[i].astype(jnp.float32)
        return carry

    lax.fori_loop(0, ranks - 1, finish, 0)

    def drain(i, carry):
        core_copy(i).wait_send()
        y_copy(i).wait_send()

        @pl.when(i < ranks - 1)
        def _():
            back_copy(i).wait_send()

        return carry

    lax.fori_loop(0, ranks, drain, 0)


def fused(
    ranks,
    coeffs,
    beta_op,
    mix_op,
    pair_op,
    send_list,
    mix_slot,
    mix_sign,
    mix_pair,
    aa_src,
    aa_sign,
    aa_pair,
):
    rows_here, beta_here = coeffs.shape
    ablk = rows_here // TILE
    bf16, f32 = jnp.bfloat16, jnp.float32
    sectors = mix_op.shape[1]
    npa = pair_op.shape[0]
    piece = (ranks, ablk, TILE, TILE)
    vmem, smem, anywhere = pltpu.VMEM, pltpu.SMEM, pl.ANY
    dma = pltpu.SemaphoreType.DMA
    result = pl.pallas_call(
        functools.partial(kernel, ranks),
        out_shape=jax.ShapeDtypeStruct((ablk, TILE, beta_here), f32),
        in_specs=[pl.BlockSpec(memory_space=anywhere)] * 3
        + [pl.BlockSpec(memory_space=vmem)]
        + [pl.BlockSpec(memory_space=smem)] * 7,
        out_specs=pl.BlockSpec(memory_space=vmem),
        scratch_shapes=[
            vmem((ranks * ablk, TILE, TILE), bf16),
            vmem((ablk, TILE, beta_here), bf16),
            vmem((beta_here, beta_here), bf16),
            vmem((sectors, TILE, TILE), bf16),
            vmem((ranks * ablk, npa, TILE, TILE), f32),
            vmem((ranks * ablk, sectors, TILE, TILE), f32),
            vmem(piece, f32),
            vmem(piece, bf16),
            vmem((ranks, 2, ablk, TILE, TILE), bf16),
            vmem((ranks, 2, ablk, TILE, TILE), bf16),
            vmem(piece, bf16),
            vmem(piece, bf16),
            vmem(piece, bf16),
            vmem(piece, bf16),
            dma((4,)),
        ]
        + [dma((ranks,))] * 8,
        compiler_params=pltpu.CompilerParams(
            collective_id=0, has_side_effects=True, vmem_limit_bytes=56 * 1024 * 1024
        ),
        cost_estimate=pl.CostEstimate(
            flops=6 * rows_here * beta_here * beta_here,
            bytes_accessed=12 * rows_here * beta_here,
            transcendentals=0,
        ),
    )(
        coeffs.reshape(ablk, TILE, beta_here),
        beta_op,
        mix_op,
        pair_op,
        jnp.transpose(send_list, (0, 2, 1)),
        mix_slot.T,
        mix_sign.T,
        mix_pair.T,
        aa_src.T,
        aa_sign.T,
        aa_pair.T,
    )
    return result.reshape(rows_here, beta_here)


def solution(mesh):
    ranks, sectors = mesh.shape["rows"], mesh.shape["sym"]

    def per_device(coeffs, *rest):
        whole_blocks = coeffs.shape[1] == ranks * TILE
        if sectors == 4 and whole_blocks:
            return fused(ranks, coeffs, *rest)
        return spread(coeffs, *rest)

    in_specs = (
        P("rows", "sym"),
        P("sym", None, None),
        P("sym", None, None, None, None),
    ) + (P(),) * 8
    return jax.shard_map(
        per_device, mesh=mesh, in_specs=in_specs, out_specs=P("rows", "sym"), check_vma=False
    )
```

```python
import functools

import jax
import jax.numpy as jnp
from jax import lax
from jax.experimental import pallas as pl
from jax.experimental.pallas import tpu as pltpu
from jax.sharding import PartitionSpec as P

TILE = 128
BT = 8
CAP = 2
NPA = 8
CHUNK = 32
MESH = pl.DeviceIdType.MESH


def spread(
    coeffs,
    beta_op,
    mix_op,
    pair_op,
    send_list,
    mix_slot,
    mix_sign,
    mix_pair,
    aa_src,
    aa_sign,
    aa_pair,
):
    rows_here, beta_here = coeffs.shape
    ablk = rows_here // TILE
    sectors = lax.axis_size("sym")
    rank_count = lax.axis_size("rows")
    sector = lax.axis_index("sym")
    my_rank = lax.axis_index("rows")
    block_count = aa_src.shape[0]
    total_rows = block_count * TILE
    col_width = beta_here // rank_count
    local_term = jnp.dot(coeffs, beta_op[0], preferred_element_type=jnp.float32)
    flipped = coeffs.T
    columns = lax.all_to_all(flipped, "rows", split_axis=0, concat_axis=1, tiled=True)
    col_blocks = columns.reshape(col_width, block_count, TILE)
    picked = jnp.take(col_blocks, aa_src, axis=1)
    operator_ids = jnp.arange(NPA, dtype=jnp.int32)
    aa_weight = (
        (1 - 2 * aa_sign)[:, :, None]
        * (aa_pair[:, :, None] == operator_ids[None, None, :]).astype(jnp.int32)
    ).astype(jnp.bfloat16)
    combined = jnp.einsum(
        "cpki,pkg->cpgi", picked, aa_weight, preferred_element_type=jnp.float32
    ).astype(jnp.bfloat16)
    alpha_part = jnp.einsum(
        "cpgj,gij->cpi", combined, pair_op, preferred_element_type=jnp.float32
    ).reshape(col_width, total_rows)
    returned = lax.all_to_all(
        alpha_part.astype(jnp.bfloat16), "rows", split_axis=1, concat_axis=0, tiled=True
    ).astype(alpha_part.dtype)
    dest_ids = jnp.arange(sectors, dtype=jnp.int32)
    pair_of = jnp.bitwise_xor(sector, dest_ids)
    operators = jnp.take(mix_op[0], pair_of, axis=0)
    sign_all = (1 - 2 * mix_sign).astype(jnp.float32)
    my_sends = lax.dynamic_index_in_dim(send_list, my_rank, 0, keepdims=False)
    blocks = coeffs.reshape(ablk, TILE, beta_here)
    taken = jnp.take(blocks, jnp.maximum(my_sends, 0), axis=0)
    outgoing = jnp.where((my_sends >= 0)[:, :, None, None], taken, jnp.zeros_like(taken))
    arrived = lax.all_to_all(outgoing, "rows", split_axis=0, concat_axis=0, tiled=True)
    slot_total = rank_count * CAP
    arrived = arrived.reshape(slot_total, TILE * beta_here)
    my_slots = lax.dynamic_slice_in_dim(mix_slot, my_rank * ablk, ablk, 0)
    my_signs = lax.dynamic_slice_in_dim(sign_all, my_rank * ablk, ablk, 0)
    my_pairs = lax.dynamic_slice_in_dim(mix_pair, my_rank * ablk, ablk, 0)
    weight = my_signs[None, :, :] * (my_pairs[None, :, :] == pair_of[:, None, None]).astype(
        jnp.float32
    )
    onehot = (
        my_slots[:, :, None] == jnp.arange(slot_total, dtype=jnp.int32)[None, None, :]
    ).astype(jnp.float32)
    mixing = (
        jnp.einsum("dpl,pls->dps", weight, onehot)
        .astype(jnp.bfloat16)
        .reshape(sectors * ablk, slot_total)
    )
    inputs = jnp.dot(mixing, arrived, preferred_element_type=jnp.float32).astype(jnp.bfloat16)
    inputs = inputs.reshape(sectors, rows_here, BT, TILE)
    products = jnp.einsum(
        "drtk,dtkj->drtj", inputs, operators, preferred_element_type=jnp.float32
    )
    mixed = lax.psum_scatter(
        products.reshape(sectors * rows_here, beta_here).astype(jnp.bfloat16),
        "sym",
        scatter_dimension=0,
        tiled=True,
    ).astype(jnp.float32)
    return local_term + returned.T + mixed


def kernel(
    ranks,
    coeffs,
    beta_op,
    mix_op,
    pair_op,
    send_list,
    mix_slot,
    mix_sign,
    mix_pair,
    aa_src,
    aa_sign,
    aa_pair,
    out,
    cols,
    mine,
    beta,
    mops,
    alphas,
    mixes,
    back_out,
    back_in,
    local_sem,
    go_send,
    go_recv,
    op_send,
    op_recv,
    y_send,
    y_recv,
    near_send,
    near_recv,
    far_send,
    far_recv,
    back_send,
    back_recv,
):
    ablk, _, beta_here = coeffs.shape
    entries = mix_slot.shape[0]
    ka = aa_src.shape[0]
    npa = pair_op.shape[0]
    sectors = mops.shape[0]
    me = lax.axis_index("rows")
    sym = lax.axis_index("sym")
    core_mate = sym + 1 - 2 * lax.rem(sym, 2)
    y_mate = lax.rem(sym + 2, 4)
    far_mate = y_mate + 1 - 2 * lax.rem(y_mate, 2)
    mates = (sym, core_mate, y_mate, far_mate)

    def block_cols(r):
        return pl.ds(pl.multiple_of(r * TILE, TILE), TILE)

    def blocks_of(r):
        return pl.ds(r * ablk, ablk)

    load_mine = pltpu.make_async_copy(coeffs, mine, local_sem.at[0])
    load_beta = pltpu.make_async_copy(beta_op.at[0], beta, local_sem.at[1])
    load_mops = pltpu.make_async_copy(mix_op.at[0, 0, me], mops.at[0], local_sem.at[2])
    load_own = pltpu.make_async_copy(
        coeffs.at[:, :, block_cols(me)], cols.at[0, blocks_of(me)], local_sem.at[3]
    )
    load_mine.start()
    load_beta.start()
    load_mops.start()
    load_own.start()

    barrier = pltpu.get_barrier_semaphore()
    for i in range(1, ranks):
        pl.semaphore_signal(
            barrier, inc=1, device_id={"rows": lax.rem(me + i, ranks)}, device_id_type=MESH
        )
    for g in range(1, sectors):
        pl.semaphore_signal(barrier, inc=1, device_id={"sym": mates[g]}, device_id_type=MESH)
    pl.semaphore_wait(barrier, ranks + sectors - 2)

    def go(i):
        r = lax.rem(me + 1 + i, ranks)
        return pltpu.make_async_remote_copy(
            src_ref=coeffs.at[:, :, block_cols(r)],
            dst_ref=cols.at[0, blocks_of(me)],
            send_sem=go_send.at[i],
            recv_sem=go_recv.at[i],
            device_id={"rows": r},
            device_id_type=MESH,
        )

    def go_in(i):
        r = lax.rem(me + 2 * ranks - 1 - i, ranks)
        return pltpu.make_async_remote_copy(
            src_ref=coeffs.at[:, :, block_cols(r)],
            dst_ref=cols.at[0, blocks_of(r)],
            send_sem=go_send.at[i],
            recv_sem=go_recv.at[i],
            device_id={"rows": r},
            device_id_type=MESH,
        )

    def op_copy(g):
        return pltpu.make_async_remote_copy(
            src_ref=mix_op.at[0, g, me],
            dst_ref=mops.at[g],
            send_sem=op_send.at[g],
            recv_sem=op_recv.at[g],
            device_id={"sym": mates[g]},
            device_id_type=MESH,
        )

    def forward(j, source, target, mate, send_sem, recv_sem):
        part = blocks_of(lax.rem(me + ranks - j, ranks))
        return pltpu.make_async_remote_copy(
            src_ref=cols.at[source, part],
            dst_ref=cols.at[target, part],
            send_sem=send_sem.at[j],
            recv_sem=recv_sem.at[j],
            device_id={"sym": mate},
            device_id_type=MESH,
        )

    def y_copy(j):
        return forward(j, 0, 2, y_mate, y_send, y_recv)

    def near_copy(j):
        return forward(j, 0, 1, core_mate, near_send, near_recv)

    def far_copy(j):
        return forward(j, 2, 3, core_mate, far_send, far_recv)

    for i in range(ranks - 1):
        go(i).start()
    load_own.wait()
    y_copy(0).start()
    near_copy(0).start()
    for g in range(1, sectors):
        op_copy(g).start()

    load_mine.wait()
    load_beta.wait()
    width = 2 * TILE

    @pl.loop(0, beta_here // width)
    def _(n):
        at = pl.ds(pl.multiple_of(n * width, width), width)

        for m in range(ablk):
            out[m, :, at] = jnp.dot(
                mine[m], beta[:, at], preferred_element_type=jnp.float32
            )

    load_mops.wait()
    for g in range(1, sectors):
        op_copy(g).wait_recv()

    def times_pairs(j):
        stacked = pair_op[...].reshape(npa * TILE, TILE)

        def one(b, carry):
            block = lax.rem(me + ranks - j, ranks) * ablk + b
            alphas[block] = jnp.dot(
                stacked, cols[0, block], preferred_element_type=jnp.float32
            ).reshape(npa, TILE, TILE)
            return carry

        lax.fori_loop(0, ablk, one, 0)

    def times_mix(j, g):
        part = blocks_of(lax.rem(me + ranks - j, ranks))
        x = cols[g, part].reshape(ablk * TILE, TILE)
        mixes[g, part] = jnp.dot(x, mops[g], preferred_element_type=jnp.float32).reshape(
            ablk, TILE, TILE
        )

    def arrive(j, carry):
        @pl.when((j >= 1) & (j < ranks))
        def _():
            go_in(j - 1).wait_recv()
            y_copy(j).start()
            near_copy(j).start()

        @pl.when(j < ranks)
        def _():
            times_pairs(j)
            times_mix(j, 0)

        @pl.when((j >= 1) & (j < ranks + 1))
        def _():
            y_copy(j - 1).wait_recv()
            far_copy(j - 1).start()
            near_copy(j - 1).wait_recv()
            times_mix(j - 1, 1)
            times_mix(j - 1, 2)

        @pl.when(j >= 2)
        def _():
            far_copy(j - 2).wait_recv()
            times_mix(j - 2, 3)

        return carry

    lax.fori_loop(0, ranks + 2, arrive, 0)

    def back_copy(i):
        return pltpu.make_async_remote_copy(
            src_ref=back_out.at[i],
            dst_ref=back_in.at[i],
            send_sem=back_send.at[i],
            recv_sem=back_recv.at[i],
            device_id={"rows": lax.rem(me + 1 + i, ranks)},
            device_id_type=MESH,
        )

    def compute(i):
        r = lax.rem(me + 1 + i, ranks)

        def one(b, carry):
            p = r * ablk + b
            picks, signs, finds, flips = [], [], [], []
            for k in range(ka):
                picks.append((aa_src[k, p], aa_pair[k, p]))
                signs.append((1 - 2 * aa_sign[k, p]).astype(jnp.float32))
            for l in range(entries):
                slot = mix_slot[l, p]
                s = lax.div(slot, CAP)
                finds.append((mix_pair[l, p], s * ablk + send_list[s, slot - s * CAP, r]))
                flips.append((1 - 2 * mix_sign[l, p]).astype(jnp.float32))
            for c in range(TILE // CHUNK):
                at = slice(c * CHUNK, (c + 1) * CHUNK)
                total = jnp.zeros((CHUNK, TILE), jnp.float32)
                for k in range(ka):
                    total = total + signs[k] * alphas[picks[k][0], picks[k][1], at, :]
                for l in range(entries):
                    total = total + flips[l] * mixes[finds[l][0], finds[l][1], at, :]
                back_out[i, b, at, :] = total.astype(jnp.bfloat16)
            return carry

        lax.fori_loop(0, ablk, one, 0)

    def step(i, carry):
        compute(i)

        @pl.when(i < ranks - 1)
        def _():
            back_copy(i).start()

        return carry

    lax.fori_loop(0, ranks, step, 0)

    at = block_cols(me)
    out[:, :, at] = out[:, :, at] + back_out[ranks - 1].astype(jnp.float32)

    def finish(i, carry):
        back_copy(i).wait_recv()
        here = block_cols(lax.rem(me + 2 * ranks - 1 - i, ranks))
        out[:, :, here] = out[:, :, here] + back_in[i].astype(jnp.float32)
        return carry

    lax.fori_loop(0, ranks - 1, finish, 0)

    def drain(i, carry):
        y_copy(i).wait_send()
        near_copy(i).wait_send()
        far_copy(i).wait_send()

        @pl.when(i < ranks - 1)
        def _():
            go(i).wait_send()
            back_copy(i).wait_send()

        return carry

    lax.fori_loop(0, ranks, drain, 0)
    for g in range(1, sectors):
        op_copy(g).wait_send()


def fused(
    ranks,
    coeffs,
    beta_op,
    mix_op,
    pair_op,
    send_list,
    mix_slot,
    mix_sign,
    mix_pair,
    aa_src,
    aa_sign,
    aa_pair,
):
    rows_here, beta_here = coeffs.shape
    ablk = rows_here // TILE
    bf16, f32 = jnp.bfloat16, jnp.float32
    sectors = mix_op.shape[1]
    npa = pair_op.shape[0]
    piece = (ranks, ablk, TILE, TILE)
    vmem, smem, anywhere = pltpu.VMEM, pltpu.SMEM, pl.ANY
    dma = pltpu.SemaphoreType.DMA
    result = pl.pallas_call(
        functools.partial(kernel, ranks),
        out_shape=jax.ShapeDtypeStruct((ablk, TILE, beta_here), f32),
        in_specs=[pl.BlockSpec(memory_space=anywhere)] * 3
        + [pl.BlockSpec(memory_space=vmem)]
        + [pl.BlockSpec(memory_space=smem)] * 7,
        out_specs=pl.BlockSpec(memory_space=vmem),
        scratch_shapes=[
            vmem((sectors, ranks * ablk, TILE, TILE), bf16),
            vmem((ablk, TILE, beta_here), bf16),
            vmem((beta_here, beta_here), bf16),
            vmem((sectors, TILE, TILE), bf16),
            vmem((ranks * ablk, npa, TILE, TILE), f32),
            vmem((sectors, ranks * ablk, TILE, TILE), f32),
            vmem(piece, bf16),
            vmem(piece, bf16),
            dma((4,)),
            dma((ranks,)),
            dma((ranks,)),
            dma((sectors,)),
            dma((sectors,)),
        ]
        + [dma((ranks,))] * 8,
        compiler_params=pltpu.CompilerParams(
            collective_id=0, has_side_effects=True, vmem_limit_bytes=56 * 1024 * 1024
        ),
        cost_estimate=pl.CostEstimate(
            flops=6 * rows_here * beta_here * beta_here,
            bytes_accessed=12 * rows_here * beta_here,
            transcendentals=0,
        ),
    )(
        coeffs.reshape(ablk, TILE, beta_here),
        beta_op,
        mix_op,
        pair_op,
        jnp.transpose(send_list, (0, 2, 1)),
        mix_slot.T,
        mix_sign.T,
        mix_pair.T,
        aa_src.T,
        aa_sign.T,
        aa_pair.T,
    )
    return result.reshape(rows_here, beta_here)


def solution(mesh):
    ranks, sectors = mesh.shape["rows"], mesh.shape["sym"]

    def per_device(coeffs, *rest):
        whole_blocks = coeffs.shape[1] == ranks * TILE
        if sectors == 4 and whole_blocks:
            return fused(ranks, coeffs, *rest)
        return spread(coeffs, *rest)

    in_specs = (
        P("rows", "sym"),
        P("sym", None, None),
        P("sym", None, None, None, None),
    ) + (P(),) * 8
    return jax.shard_map(
        per_device, mesh=mesh, in_specs=in_specs, out_specs=P("rows", "sym"), check_vma=False
    )
```

```python
import functools

import jax
import jax.numpy as jnp
from jax import lax
from jax.experimental import pallas as pl
from jax.experimental.pallas import tpu as pltpu
from jax.sharding import PartitionSpec as P

TILE = 128
BT = 8
CAP = 2
NPA = 8
CHUNK = 32
MESH = pl.DeviceIdType.MESH


def spread(
    coeffs,
    beta_op,
    mix_op,
    pair_op,
    send_list,
    mix_slot,
    mix_sign,
    mix_pair,
    aa_src,
    aa_sign,
    aa_pair,
):
    rows_here, beta_here = coeffs.shape
    ablk = rows_here // TILE
    sectors = lax.axis_size("sym")
    rank_count = lax.axis_size("rows")
    sector = lax.axis_index("sym")
    my_rank = lax.axis_index("rows")
    block_count = aa_src.shape[0]
    total_rows = block_count * TILE
    col_width = beta_here // rank_count
    local_term = jnp.dot(coeffs, beta_op[0], preferred_element_type=jnp.float32)
    flipped = coeffs.T
    columns = lax.all_to_all(flipped, "rows", split_axis=0, concat_axis=1, tiled=True)
    col_blocks = columns.reshape(col_width, block_count, TILE)
    picked = jnp.take(col_blocks, aa_src, axis=1)
    operator_ids = jnp.arange(NPA, dtype=jnp.int32)
    aa_weight = (
        (1 - 2 * aa_sign)[:, :, None]
        * (aa_pair[:, :, None] == operator_ids[None, None, :]).astype(jnp.int32)
    ).astype(jnp.bfloat16)
    combined = jnp.einsum(
        "cpki,pkg->cpgi", picked, aa_weight, preferred_element_type=jnp.float32
    ).astype(jnp.bfloat16)
    alpha_part = jnp.einsum(
        "cpgj,gij->cpi", combined, pair_op, preferred_element_type=jnp.float32
    ).reshape(col_width, total_rows)
    returned = lax.all_to_all(
        alpha_part.astype(jnp.bfloat16), "rows", split_axis=1, concat_axis=0, tiled=True
    ).astype(alpha_part.dtype)
    dest_ids = jnp.arange(sectors, dtype=jnp.int32)
    pair_of = jnp.bitwise_xor(sector, dest_ids)
    operators = jnp.take(mix_op[0], pair_of, axis=0)
    sign_all = (1 - 2 * mix_sign).astype(jnp.float32)
    my_sends = lax.dynamic_index_in_dim(send_list, my_rank, 0, keepdims=False)
    blocks = coeffs.reshape(ablk, TILE, beta_here)
    taken = jnp.take(blocks, jnp.maximum(my_sends, 0), axis=0)
    outgoing = jnp.where((my_sends >= 0)[:, :, None, None], taken, jnp.zeros_like(taken))
    arrived = lax.all_to_all(outgoing, "rows", split_axis=0, concat_axis=0, tiled=True)
    slot_total = rank_count * CAP
    arrived = arrived.reshape(slot_total, TILE * beta_here)
    my_slots = lax.dynamic_slice_in_dim(mix_slot, my_rank * ablk, ablk, 0)
    my_signs = lax.dynamic_slice_in_dim(sign_all, my_rank * ablk, ablk, 0)
    my_pairs = lax.dynamic_slice_in_dim(mix_pair, my_rank * ablk, ablk, 0)
    weight = my_signs[None, :, :] * (my_pairs[None, :, :] == pair_of[:, None, None]).astype(
        jnp.float32
    )
    onehot = (
        my_slots[:, :, None] == jnp.arange(slot_total, dtype=jnp.int32)[None, None, :]
    ).astype(jnp.float32)
    mixing = (
        jnp.einsum("dpl,pls->dps", weight, onehot)
        .astype(jnp.bfloat16)
        .reshape(sectors * ablk, slot_total)
    )
    inputs = jnp.dot(mixing, arrived, preferred_element_type=jnp.float32).astype(jnp.bfloat16)
    inputs = inputs.reshape(sectors, rows_here, BT, TILE)
    products = jnp.einsum(
        "drtk,dtkj->drtj", inputs, operators, preferred_element_type=jnp.float32
    )
    mixed = lax.psum_scatter(
        products.reshape(sectors * rows_here, beta_here).astype(jnp.bfloat16),
        "sym",
        scatter_dimension=0,
        tiled=True,
    ).astype(jnp.float32)
    return local_term + returned.T + mixed


def kernel(
    ranks,
    coeffs,
    beta_op,
    mix_op,
    pair_op,
    send_list,
    mix_slot,
    mix_sign,
    mix_pair,
    aa_src,
    aa_sign,
    aa_pair,
    local,
    back,
    out,
    cols,
    mine,
    beta,
    mops,
    alphas,
    mixes,
    back_out,
    local_sem,
    go_send,
    go_recv,
    op_send,
    op_recv,
    y_send,
    y_recv,
    near_send,
    near_recv,
    far_send,
    far_recv,
    back_send,
    back_recv,
):
    ablk, _, beta_here = coeffs.shape
    entries = mix_slot.shape[0]
    ka = aa_src.shape[0]
    npa = pair_op.shape[0]
    sectors = mops.shape[0]
    me = lax.axis_index("rows")
    sym = lax.axis_index("sym")
    core_mate = sym + 1 - 2 * lax.rem(sym, 2)
    y_mate = lax.rem(sym + 2, 4)
    far_mate = y_mate + 1 - 2 * lax.rem(y_mate, 2)
    mates = (sym, core_mate, y_mate, far_mate)

    def shift(i):
        return ranks // 2 + lax.div(i + 1, 2) * (2 * lax.rem(i, 2) - 1)

    def target(i):
        return lax.rem(me + shift(i), ranks)

    def origin(i):
        return lax.rem(me + ranks - shift(i), ranks)

    def held(j):
        return origin(lax.rem(j + ranks - 1, ranks))

    def block_cols(r):
        return pl.ds(pl.multiple_of(r * TILE, TILE), TILE)

    def blocks_of(r):
        return pl.ds(r * ablk, ablk)

    load_mine = pltpu.make_async_copy(coeffs, mine, local_sem.at[0])
    load_beta = pltpu.make_async_copy(beta_op.at[0], beta, local_sem.at[1])
    load_mops = pltpu.make_async_copy(mix_op.at[0, 0, me], mops.at[0], local_sem.at[2])
    load_own = pltpu.make_async_copy(
        coeffs.at[:, :, block_cols(me)], cols.at[0, blocks_of(me)], local_sem.at[3]
    )
    load_mine.start()
    load_beta.start()
    load_mops.start()
    load_own.start()

    barrier = pltpu.get_barrier_semaphore()
    for i in range(1, ranks):
        pl.semaphore_signal(
            barrier, inc=1, device_id={"rows": lax.rem(me + i, ranks)}, device_id_type=MESH
        )
    for g in range(1, sectors):
        pl.semaphore_signal(barrier, inc=1, device_id={"sym": mates[g]}, device_id_type=MESH)
    pl.semaphore_wait(barrier, ranks + sectors - 2)

    def go(i):
        r = target(i)
        return pltpu.make_async_remote_copy(
            src_ref=coeffs.at[:, :, block_cols(r)],
            dst_ref=cols.at[0, blocks_of(me)],
            send_sem=go_send.at[i],
            recv_sem=go_recv.at[i],
            device_id={"rows": r},
            device_id_type=MESH,
        )

    def go_in(i):
        r = origin(i)
        return pltpu.make_async_remote_copy(
            src_ref=coeffs.at[:, :, block_cols(r)],
            dst_ref=cols.at[0, blocks_of(r)],
            send_sem=go_send.at[i],
            recv_sem=go_recv.at[i],
            device_id={"rows": r},
            device_id_type=MESH,
        )

    def op_copy(g):
        return pltpu.make_async_remote_copy(
            src_ref=mix_op.at[0, g, me],
            dst_ref=mops.at[g],
            send_sem=op_send.at[g],
            recv_sem=op_recv.at[g],
            device_id={"sym": mates[g]},
            device_id_type=MESH,
        )

    def forward(j, source, goal, mate, send_sem, recv_sem):
        part = blocks_of(held(j))
        return pltpu.make_async_remote_copy(
            src_ref=cols.at[source, part],
            dst_ref=cols.at[goal, part],
            send_sem=send_sem.at[j],
            recv_sem=recv_sem.at[j],
            device_id={"sym": mate},
            device_id_type=MESH,
        )

    def y_copy(j):
        return forward(j, 0, 2, y_mate, y_send, y_recv)

    def near_copy(j):
        return forward(j, 0, 1, core_mate, near_send, near_recv)

    def far_copy(j):
        return forward(j, 2, 3, core_mate, far_send, far_recv)

    for i in range(ranks - 1):
        go(i).start()
    load_own.wait()
    y_copy(0).start()
    near_copy(0).start()
    for g in range(1, sectors):
        op_copy(g).start()

    load_mine.wait()
    load_beta.wait()
    width = 2 * TILE

    @pl.loop(0, beta_here // width)
    def _(n):
        at = pl.ds(pl.multiple_of(n * width, width), width)

        for m in range(ablk):
            out[m, :, at] = jnp.dot(
                mine[m], beta[:, at], preferred_element_type=jnp.float32
            )

    save = pltpu.make_async_copy(out, local, local_sem.at[0])
    save.start()
    load_mops.wait()
    for g in range(1, sectors):
        op_copy(g).wait_recv()

    def times_pairs(j):
        stacked = pair_op[...].reshape(npa * TILE, TILE)

        def one(b, carry):
            block = held(j) * ablk + b
            alphas[block] = jnp.dot(
                stacked, cols[0, block], preferred_element_type=jnp.float32
            ).reshape(npa, TILE, TILE)
            return carry

        lax.fori_loop(0, ablk, one, 0)

    def times_mix(j, g):
        part = blocks_of(held(j))
        x = cols[g, part].reshape(ablk * TILE, TILE)
        mixes[g, part] = jnp.dot(x, mops[g], preferred_element_type=jnp.float32).reshape(
            ablk, TILE, TILE
        )

    def arrive(j, carry):
        @pl.when((j >= 1) & (j < ranks))
        def _():
            go_in(j - 1).wait_recv()
            y_copy(j).start()
            near_copy(j).start()

        @pl.when(j < ranks)
        def _():
            times_pairs(j)
            times_mix(j, 0)

        @pl.when((j >= 1) & (j < ranks + 1))
        def _():
            y_copy(j - 1).wait_recv()
            far_copy(j - 1).start()
            near_copy(j - 1).wait_recv()
            times_mix(j - 1, 1)
            times_mix(j - 1, 2)

        @pl.when(j >= 2)
        def _():
            far_copy(j - 2).wait_recv()
            times_mix(j - 2, 3)

        return carry

    lax.fori_loop(0, ranks + 2, arrive, 0)

    def back_copy(i):
        return pltpu.make_async_remote_copy(
            src_ref=back_out.at[i],
            dst_ref=back.at[me],
            send_sem=back_send.at[i],
            recv_sem=back_recv.at[i],
            device_id={"rows": target(i)},
            device_id_type=MESH,
        )

    def back_arrival(i):
        return pltpu.make_async_remote_copy(
            src_ref=back_out.at[i],
            dst_ref=back.at[origin(i)],
            send_sem=back_send.at[i],
            recv_sem=back_recv.at[i],
            device_id={"rows": origin(i)},
            device_id_type=MESH,
        )

    def compute(i):
        r = target(i)

        def one(b, carry):
            p = r * ablk + b
            picks, signs, finds, flips = [], [], [], []
            for k in range(ka):
                picks.append((aa_src[k, p], aa_pair[k, p]))
                signs.append((1 - 2 * aa_sign[k, p]).astype(jnp.float32))
            for l in range(entries):
                slot = mix_slot[l, p]
                s = lax.div(slot, CAP)
                finds.append((mix_pair[l, p], s * ablk + send_list[s, slot - s * CAP, r]))
                flips.append((1 - 2 * mix_sign[l, p]).astype(jnp.float32))
            for c in range(TILE // CHUNK):
                at = slice(c * CHUNK, (c + 1) * CHUNK)
                total = jnp.zeros((CHUNK, TILE), jnp.float32)
                for k in range(ka):
                    total = total + signs[k] * alphas[picks[k][0], picks[k][1], at, :]
                for l in range(entries):
                    total = total + flips[l] * mixes[finds[l][0], finds[l][1], at, :]
                back_out[i, b, at, :] = total.astype(jnp.bfloat16)
            return carry

        lax.fori_loop(0, ablk, one, 0)

    def step(i, carry):
        compute(i)

        @pl.when(i < ranks - 1)
        def _():
            back_copy(i).start()

        return carry

    lax.fori_loop(0, ranks, step, 0)

    keep_own = pltpu.make_async_copy(back_out.at[ranks - 1], back.at[me], local_sem.at[3])
    keep_own.start()

    def finish(i, carry):
        back_arrival(i).wait_recv()
        return carry

    lax.fori_loop(0, ranks - 1, finish, 0)
    keep_own.wait()
    save.wait()

    def drain(i, carry):
        y_copy(i).wait_send()
        near_copy(i).wait_send()
        far_copy(i).wait_send()

        @pl.when(i < ranks - 1)
        def _():
            go(i).wait_send()
            back_copy(i).wait_send()

        return carry

    lax.fori_loop(0, ranks, drain, 0)
    for g in range(1, sectors):
        op_copy(g).wait_send()


def add(local, back, out):
    for t in range(back.shape[0]):
        at = slice(t * TILE, (t + 1) * TILE)
        out[0, :, at] = local[0, :, at] + back[t, 0].astype(jnp.float32)


def fused(
    ranks,
    coeffs,
    beta_op,
    mix_op,
    pair_op,
    send_list,
    mix_slot,
    mix_sign,
    mix_pair,
    aa_src,
    aa_sign,
    aa_pair,
):
    rows_here, beta_here = coeffs.shape
    ablk = rows_here // TILE
    bf16, f32 = jnp.bfloat16, jnp.float32
    sectors = mix_op.shape[1]
    npa = pair_op.shape[0]
    piece = (ranks, ablk, TILE, TILE)
    vmem, smem, anywhere = pltpu.VMEM, pltpu.SMEM, pl.ANY
    dma = pltpu.SemaphoreType.DMA
    local, back = pl.pallas_call(
        functools.partial(kernel, ranks),
        out_shape=(
            jax.ShapeDtypeStruct((ablk, TILE, beta_here), f32),
            jax.ShapeDtypeStruct(piece, bf16),
        ),
        in_specs=[pl.BlockSpec(memory_space=anywhere)] * 3
        + [pl.BlockSpec(memory_space=vmem)]
        + [pl.BlockSpec(memory_space=smem)] * 7,
        out_specs=(pl.BlockSpec(memory_space=anywhere),) * 2,
        scratch_shapes=[
            vmem((ablk, TILE, beta_here), f32),
            vmem((sectors, ranks * ablk, TILE, TILE), bf16),
            vmem((ablk, TILE, beta_here), bf16),
            vmem((beta_here, beta_here), bf16),
            vmem((sectors, TILE, TILE), bf16),
            vmem((ranks * ablk, npa, TILE, TILE), f32),
            vmem((sectors, ranks * ablk, TILE, TILE), f32),
            vmem(piece, bf16),
            dma((4,)),
            dma((ranks,)),
            dma((ranks,)),
            dma((sectors,)),
            dma((sectors,)),
        ]
        + [dma((ranks,))] * 8,
        compiler_params=pltpu.CompilerParams(
            collective_id=0, has_side_effects=True, vmem_limit_bytes=56 * 1024 * 1024
        ),
        cost_estimate=pl.CostEstimate(
            flops=6 * rows_here * beta_here * beta_here,
            bytes_accessed=12 * rows_here * beta_here,
            transcendentals=0,
        ),
    )(
        coeffs.reshape(ablk, TILE, beta_here),
        beta_op,
        mix_op,
        pair_op,
        jnp.transpose(send_list, (0, 2, 1)),
        mix_slot.T,
        mix_sign.T,
        mix_pair.T,
        aa_src.T,
        aa_sign.T,
        aa_pair.T,
    )
    result = pl.pallas_call(
        add,
        grid=(ablk,),
        out_shape=jax.ShapeDtypeStruct((ablk, TILE, beta_here), f32),
        in_specs=[
            pl.BlockSpec((1, TILE, beta_here), lambda b: (b, 0, 0)),
            pl.BlockSpec((ranks, 1, TILE, TILE), lambda b: (0, b, 0, 0)),
        ],
        out_specs=pl.BlockSpec((1, TILE, beta_here), lambda b: (b, 0, 0)),
    )(local, back)
    return result.reshape(rows_here, beta_here)


def solution(mesh):
    ranks, sectors = mesh.shape["rows"], mesh.shape["sym"]

    def per_device(coeffs, *rest):
        whole_blocks = coeffs.shape[1] == ranks * TILE
        if sectors == 4 and ranks % 2 == 0 and whole_blocks:
            return fused(ranks, coeffs, *rest)
        return spread(coeffs, *rest)

    in_specs = (
        P("rows", "sym"),
        P("sym", None, None),
        P("sym", None, None, None, None),
    ) + (P(),) * 8
    return jax.shard_map(
        per_device, mesh=mesh, in_specs=in_specs, out_specs=P("rows", "sym"), check_vma=False
    )
```
